512 devices in a mesh: section: 8 (over z_hi, core), tensor: 8 (over x, z_lo), dp: 8 (over y).
Axes of the slice: x: 4, y: 8, z: 8 (z_hi: 4, z_lo: 2; z = z_hi * 2 + z_lo), core: 2. Of those that a mesh axis runs over, the one named last changes fastest.
Arguments:
- activations: bfloat16 [8, 16, 64, 4096], P('section', 'dp', None, 'tensor')
- cotangent: bfloat16 [16, 64, 4096], P('dp', None, 'tensor'), may hold values from -6 to 6
- lengths: int32 [16], P('dp'), may hold values from 16 to 64
- weights: bfloat16 [8, 4096, 4096], P('section', 'tensor', 'dp'), may hold values from -0.0625 to 0.0625
- gains: bfloat16 [8, 4096], P('section', 'tensor'), may hold values from 0.25 to 1.75
Outputs:
- input_grads: bfloat16 [8, 16, 64, 4096], P('section', 'dp', None, 'tensor')
- weight_grads: float32 [8, 4096, 4096], P('section', 'tensor', 'dp')
- gain_grads: float32 [8, 4096], P('section', 'tensor')
The draws below stay inside these ranges and needn't reach their ends.
All inputs are finite; a program needn't handle non-finite values.
Results may differ from the reference program's by a relative error of at most 0.022.
Values may be sent and summed in bfloat16 or wider, within the bound.
A program may use at most 64 MiB of HBM per device.

```python
import math
import jax
import jax.numpy as jnp
from jax import lax

MODEL_WIDTH = 4096
MB = 2
SEQ = 64
BATCH = 16
SECTIONS = 8
N_DP = 8


def draw_activations(key, part):
    key = jax.random.fold_in(key, 11)
    key_base, key_rows, key_cols = jax.random.split(key, 3)
    shape = (SECTIONS, BATCH, SEQ, MODEL_WIDTH)
    rows = jnp.exp(jax.random.uniform(key_rows, (SECTIONS, BATCH, SEQ, 1), jnp.float32, math.log(0.3), math.log(3.0)))
    cols = jnp.exp(jax.random.uniform(key_cols, (1, 1, 1, MODEL_WIDTH), jnp.float32, math.log(0.5), math.log(2.0)))
    base = jax.random.normal(key_base, shape, jnp.float32)
    return (base * rows * cols).astype(jnp.bfloat16)


def set_ends(entries, rng, smallest, high):
    longest = entries.shape.index(max(entries.shape))
    spots = []
    for shift in (0, 1):
        where = [jax.random.randint(jax.random.fold_in(rng, axis), (), 0, length) for axis, length in enumerate(entries.shape)]
        where[longest] = (where[longest] + shift) % entries.shape[longest]
        spots.append(tuple(where))
    return entries.at[spots[0]].set(smallest).at[spots[1]].set(high)


def block_levels(stream_key, shape, pieces, smallest, largest):
    factor_of, own = 1.0, jax.random.fold_in(stream_key, 6)
    for position, parts in pieces:
        heights = jnp.exp(jax.random.uniform(jax.random.fold_in(own, position), (parts,), jnp.float32, smallest / len(pieces), largest / len(pieces)))
        factor_of = factor_of * jnp.repeat(heights, shape[position] // parts).reshape([-1 if axis == position else 1 for axis in range(len(shape))])
    return factor_of


def centred(own_key, extent, deviation, reach, shards=(), kind=jnp.bfloat16):
    loudness = block_levels(own_key, extent, shards, -0.22, 0.18) if shards else 1.0
    drawn = jax.random.normal(own_key, extent, jnp.float32) * deviation * loudness
    return jnp.minimum(jnp.maximum(drawn, -reach), reach).astype(kind)


def setup_inputs(seed: int = 0) -> dict:
    arg_keys = jax.random.split(jax.random.key(seed), 6)
    activations = draw_activations(jax.random.fold_in(arg_keys[5], 71), 0)
    cotangent = centred(arg_keys[1], (BATCH, SEQ, MODEL_WIDTH), 1.0, 6.0, ((0, 8), (2, 8)))
    lengths = set_ends(jax.random.randint(arg_keys[2], (BATCH,), SEQ // 4, SEQ + 1), jax.random.fold_in(arg_keys[2], 1), SEQ // 4, SEQ).astype(jnp.int32)
    weights = centred(arg_keys[3], (SECTIONS, MODEL_WIDTH, MODEL_WIDTH), (2 * MODEL_WIDTH) ** -0.5, 0.0625, ((0, 8), (1, 8), (2, 8)))
    gains = jnp.clip(1.0 + 0.15 * jax.random.normal(arg_keys[4], (SECTIONS, MODEL_WIDTH), jnp.float32), 0.25, 1.75).astype(jnp.bfloat16)
    return {"activations": activations, "cotangent": cotangent, "lengths": lengths, "weights": weights, "gains": gains}


eps = 1e-05

def reference(activations, cotangent, lengths, weights, gains):
    input_rows = activations.astype(jnp.float32)
    inverse_scale = lax.rsqrt(lax.optimization_barrier(jnp.mean(input_rows * input_rows, axis=-1)) + eps)
    centered_input = input_rows * inverse_scale[..., None]
    gain_stacked = gains.astype(jnp.float32)
    normalized_rows = (centered_input * gain_stacked[:, None, None, :]).astype(jnp.bfloat16)
    positions = jnp.arange(SEQ, dtype=jnp.int32)
    keep = positions[None, :] < lengths[:, None]
    running_gradient = jnp.where(keep[..., None], cotangent, jnp.zeros_like(cotangent)).astype(jnp.bfloat16)
    grads_list = [None] * SECTIONS
    weight_list = [None] * SECTIONS
    gain_sequence = [None] * SECTIONS
    for section_index in reversed(range(SECTIONS)):
        flat_grad = running_gradient.reshape(BATCH * SEQ, MODEL_WIDTH)
        backward_signal = jnp.dot(flat_grad, weights[section_index].T, preferred_element_type=jnp.float32).reshape(BATCH, SEQ, MODEL_WIDTH)
        gain_weighted = gain_stacked[section_index] * backward_signal
        row_correction = lax.optimization_barrier(jnp.sum(gain_weighted * centered_input[section_index], axis=-1)) / MODEL_WIDTH
        loss_total = running_gradient.astype(jnp.float32) + inverse_scale[section_index][..., None] * (gain_weighted - centered_input[section_index] * row_correction[..., None])
        grads_list[section_index] = loss_total.astype(jnp.bfloat16)
        normed_rep = normalized_rows[section_index].reshape(N_DP, MB * SEQ, MODEL_WIDTH)
        grad_rep = running_gradient.reshape(N_DP, MB * SEQ, MODEL_WIDTH)
        accum = jnp.zeros((MODEL_WIDTH, MODEL_WIDTH), jnp.float32)
        for replica in range(N_DP):
            partial_value = jnp.dot(normed_rep[replica].T, grad_rep[replica], preferred_element_type=jnp.float32)
            accum = accum + lax.optimization_barrier(partial_value.astype(jnp.bfloat16)).astype(jnp.float32)
        weight_list[section_index] = accum
        gain_sequence[section_index] = lax.optimization_barrier(jnp.sum(backward_signal * centered_input[section_index], axis=(0, 1)))
        running_gradient = grads_list[section_index]
    return (jnp.stack(grads_list), jnp.stack(weight_list), jnp.stack(gain_sequence))
```

```python
import functools

import jax
import jax.numpy as jnp
from jax import lax
from jax.experimental import pallas as pl
from jax.experimental.pallas import tpu as pltpu
from jax.sharding import PartitionSpec as P

EPS = 1e-05
LANES = 128
CHUNKS = 4
PIECES = 4
MESH = pl.DeviceIdType.MESH


def remote(src, dst, send, recv, dev):
    return pltpu.make_async_remote_copy(
        src_ref=src, dst_ref=dst, send_sem=send, recv_sem=recv, device_id=dev, device_id_type=MESH
    )


def wide(tile, cols):
    return jnp.concatenate([tile] * (cols // LANES), axis=1)


def kernel(
    sizes,
    lengths_ref, x_ref, cot_ref, w_ref, gain_ref,
    grads_out, wgrad_out, gain_out,
    w_all, inbox, grad_all, corr, corr_own, normed_all, swapped, xhat, upd, outbox,
    squares, rterm, gain_part,
    w_send, w_recv, relay_send, relay_recv, swap_send, swap_recv,
    sq_send, sq_recv, corr_send, corr_recv, norm_send, norm_recv,
    r_send, r_recv, gn_send, gn_recv,
):
    ns, nt, nd = sizes
    s, t, d = lax.axis_index("section"), lax.axis_index("tensor"), lax.axis_index("dp")
    tokens, cols = x_ref.shape
    width = cols * nt
    rows = tokens // CHUNKS
    seqlen = tokens // 2
    first, last = s == ns - 1, s == 0
    dp_peer = lambda k: lax.rem(d + k, nd)
    t_peer = lambda k: lax.rem(t + k, nt)

    barrier = pltpu.get_barrier_semaphore()
    for k in range(1, nd):
        pl.semaphore_signal(barrier, 1, device_id={"dp": dp_peer(k)}, device_id_type=MESH)
    for k in range(1, nt):
        pl.semaphore_signal(barrier, 1, device_id={"tensor": t_peer(k)}, device_id_type=MESH)

    @pl.when(jnp.logical_not(last))
    def _():
        for k in range(nt):
            pl.semaphore_signal(
                barrier, 1, device_id={"section": s - 1, "tensor": t_peer(k)}, device_id_type=MESH
            )

    @pl.when(jnp.logical_not(first))
    def _():
        for k in range(nt):
            pl.semaphore_signal(
                barrier, 1, device_id={"section": s + 1, "tensor": t_peer(k)}, device_id_type=MESH
            )

    w_all[d] = w_ref[...].T
    x = x_ref[...].astype(jnp.float32)
    squares[t] = jnp.broadcast_to(jnp.sum(x * x, axis=1, keepdims=True), (tokens, LANES))

    @pl.when(first)
    def _():
        position = lax.broadcasted_iota(jnp.int32, (seqlen, cols), 0)
        for m in range(2):
            part = slice(m * seqlen, (m + 1) * seqlen)
            masked = jnp.where(
                position < lengths_ref[m], cot_ref[part, :].astype(jnp.float32), 0.0
            ).astype(jnp.bfloat16)
            outbox[part, :cols] = masked
            inbox[t, part, :cols] = masked
        outbox[:, cols:] = jnp.zeros((tokens, LANES), jnp.bfloat16)
        inbox[t, :, cols:] = jnp.zeros((tokens, LANES), jnp.bfloat16)
        corr[...] = jnp.zeros_like(corr)

    expected = nd - 1 + nt - 1 + nt * (
        jnp.where(last, 0, 1) + jnp.where(first, 0, 1)
    )
    pl.semaphore_wait(barrier, expected)

    size = cols // PIECES

    def w_copy(hop, piece, way):
        block = lax.rem(d - way * (hop - 1) + 2 * nd, nd)
        view = w_all.at[block, pl.ds(piece * size, size)]
        side = 0 if way > 0 else 1
        return remote(
            view, view, w_send.at[side, hop - 1, piece], w_recv.at[side, hop - 1, piece],
            {"dp": lax.rem(d + way + nd, nd)},
        )

    def w_arrived(hop, piece, way):
        block = lax.rem(d - way * hop + 2 * nd, nd)
        view = w_all.at[block, pl.ds(piece * size, size)]
        side = 0 if way > 0 else 1
        remote(
            view, view, w_send.at[side, hop - 1, piece], w_recv.at[side, hop - 1, piece],
            {"dp": lax.rem(d + way + nd, nd)},
        ).wait_recv()

    half = PIECES // 2
    hops = nd // 2
    travels = lambda hop, piece, way: hop < hops or (piece < half) == (way > 0)

    def w_hop(hop):
        for piece in range(PIECES):
            for way in (1, -1):
                if travels(hop, piece, way):
                    if hop > 1:
                        w_arrived(hop - 1, piece, way)
                    w_copy(hop, piece, way).start()

    w_hop(1)

    def sq_copy(k, src):
        return remote(
            squares.at[src], squares.at[src], sq_send.at[k], sq_recv.at[src], {"tensor": t_peer(k)}
        )

    for k in range(1, nt):
        sq_copy(k, t).start()

    def first_copy(c, k):
        view = pl.ds(c * rows, rows)
        return remote(
            outbox.at[view], inbox.at[t, view], relay_send.at[c, k], relay_recv.at[c, t],
            {"tensor": t_peer(k)},
        )

    def relay_copy(c, k):
        view = pl.ds(c * rows, rows)
        return remote(
            outbox.at[view], inbox.at[t, view], relay_send.at[c, k], relay_recv.at[c, t],
            {"section": s - 1, "tensor": t_peer(k)},
        )

    @pl.when(first)
    def _():
        for c in range(CHUNKS):
            for k in range(1, nt):
                first_copy(c, k).start()

    for k in range(1, nt):
        sq_copy(k, t_peer(k)).wait_recv()
    total = squares[0]
    for j in range(1, nt):
        total = total + squares[j]
    scale = wide(lax.rsqrt(total / width + EPS), cols)
    gain = gain_ref[...].astype(jnp.float32)
    x = x_ref[...].astype(jnp.float32) * scale
    xhat[...] = x
    normed_all[d] = (x * gain).astype(jnp.bfloat16)
    corr_own[...] = (x * scale).astype(jnp.bfloat16)
    upd[...] = scale

    def corr_copy(k):
        return remote(
            corr_own, corr.at[t], corr_send.at[k], corr_recv.at[t],
            {"section": s - 1, "tensor": t_peer(k)},
        )

    @pl.when(jnp.logical_not(last))
    def _():
        for k in range(nt):
            corr_copy(k).start()

    for hop in range(2, hops + 1):
        w_hop(hop)
    for hop in range(hops - 1, hops + 1):
        for piece in range(PIECES):
            for way in (1, -1):
                if travels(hop, piece, way) and not travels(hop + 1, piece, way) or hop == hops and travels(hop, piece, way):
                    w_arrived(hop, piece, way)

    def norm_copy(k, src):
        return remote(
            normed_all.at[src], normed_all.at[src], norm_send.at[k], norm_recv.at[src],
            {"dp": dp_peer(k)},
        )

    for k in range(1, nd):
        norm_copy(k, d).start()

    @pl.when(jnp.logical_not(first))
    def _():
        for k in range(nt):
            src = t_peer(k)
            remote(
                corr_own, corr.at[src], corr_send.at[k], corr_recv.at[src], {"tensor": t_peer(1)}
            ).wait_recv()

    gain_part[d] = jnp.zeros((8, cols), jnp.float32)

    def relay_arrived(c, k):
        src = t_peer(k)
        view = pl.ds(c * rows, rows)
        remote(
            outbox.at[view], inbox.at[src, view], relay_send.at[c, k], relay_recv.at[c, src],
            {"tensor": t_peer(1)},
        ).wait_recv()

    def swap_copy(c, k):
        view = pl.ds(pl.multiple_of(c * rows, rows), rows)
        return remote(
            grad_all.at[dp_peer(k), view], swapped.at[d, view], swap_send.at[c, k],
            swap_recv.at[c, d], {"dp": dp_peer(k)},
        )

    def swap_arrived(c, k):
        src = dp_peer(k)
        view = pl.ds(pl.multiple_of(c * rows, rows), rows)
        remote(
            grad_all.at[src, view], swapped.at[src, view], swap_send.at[c, k],
            swap_recv.at[c, src], {"dp": dp_peer(1)},
        ).wait_recv()

    def chunk(c, carry):
        view = pl.ds(pl.multiple_of(c * rows, rows), rows)

        @pl.when(jnp.logical_not(first))
        def _():
            relay_arrived(c, 0)

        for k in range(1, nt):
            relay_arrived(c, k)
        r = inbox[0, view, cols:].astype(jnp.float32)
        for j in range(1, nt):
            r = r + inbox[j, view, cols:].astype(jnp.float32)
        r = wide(r, cols)
        back = jnp.zeros((rows, cols), jnp.float32)
        for j in range(nt):
            g = inbox[j, view, :cols].astype(jnp.float32) - corr[j, view].astype(jnp.float32) * r
            g = g.astype(jnp.bfloat16)
            grad_all[j, view] = g
            back = back + jnp.dot(g, w_all[j], preferred_element_type=jnp.float32)
        xh = xhat[view]
        weighted = gain * back
        part = jnp.sum(weighted * xh, axis=1, keepdims=True) * (1.0 / width)
        u = grad_all[t, view].astype(jnp.float32) + upd[view] * weighted
        outbox[view, :cols] = u.astype(jnp.bfloat16)
        tile = jnp.broadcast_to(part, (rows, LANES)).astype(jnp.bfloat16)
        outbox[view, cols:] = tile

        @pl.when(jnp.logical_not(last))
        def _():
            for k in range(nt):
                relay_copy(c, k).start()

        for k in range(1, nd):
            swap_copy(c, k).start()
        swapped[d, view] = grad_all[d, view]
        upd[view] = u
        rterm[t, view] = tile
        gain_part[d] = gain_part[d] + jnp.sum((back * xh).reshape(rows // 8, 8, cols), axis=0)
        return carry

    @pl.when(first)
    def _():
        for c in range(CHUNKS):
            for k in range(1, nt):
                first_copy(c, k).wait_send()

    lax.fori_loop(0, CHUNKS, chunk, 0)

    def r_copy(k, src):
        return remote(rterm.at[src], rterm.at[src], r_send.at[k], r_recv.at[src], {"tensor": t_peer(k)})

    def gn_copy(k, src):
        return remote(
            gain_part.at[src], gain_part.at[src], gn_send.at[k], gn_recv.at[src], {"dp": dp_peer(k)}
        )

    for k in range(1, nt):
        r_copy(k, t).start()
    for k in range(1, nd):
        gn_copy(k, d).start()
    for k in range(1, nt):
        r_copy(k, t_peer(k)).wait_recv()
    r = rterm[0].astype(jnp.float32)
    for j in range(1, nt):
        r = r + rterm[j].astype(jnp.float32)
    grads_out[...] = (
        upd[...] - corr_own[...].astype(jnp.float32) * wide(r, cols)
    ).astype(jnp.bfloat16)
    for k in range(1, nd):
        gn_copy(k, dp_peer(k)).wait_recv()
    sums = gain_part[0]
    for j in range(1, nd):
        sums = sums + gain_part[j]
    gain_out[...] = jnp.sum(sums, axis=0, keepdims=True)

    for k in range(1, nd):
        norm_copy(k, dp_peer(k)).wait_recv()
        for c in range(CHUNKS):
            swap_arrived(c, k)
    acc = jnp.zeros((cols, cols), jnp.float32)
    for j in range(nd):
        acc = acc + lax.dot_general(
            normed_all[j], swapped[j], (((0,), (0,)), ((), ())), preferred_element_type=jnp.float32
        )
    wgrad_out[...] = acc

    for hop in range(1, hops + 1):
        for piece in range(PIECES):
            for way in (1, -1):
                if travels(hop, piece, way):
                    w_copy(hop, piece, way).wait_send()
    for k in range(1, nt):
        sq_copy(k, t).wait_send()
        r_copy(k, t).wait_send()
    for k in range(1, nd):
        norm_copy(k, d).wait_send()
        gn_copy(k, d).wait_send()
        for c in range(CHUNKS):
            swap_copy(c, k).wait_send()

    @pl.when(jnp.logical_not(last))
    def _():
        for k in range(nt):
            corr_copy(k).wait_send()
            for c in range(CHUNKS):
                relay_copy(c, k).wait_send()


def per_device(activations, cotangent, lengths, weights, gains):
    ns, nt, nd = (lax.axis_size(a) for a in ("section", "tensor", "dp"))
    _, micro, seqlen, cols = activations.shape
    tokens = micro * seqlen
    bf16, f32 = jnp.bfloat16, jnp.float32
    vmem = pl.BlockSpec(memory_space=pltpu.VMEM)
    dma = lambda *shape: pltpu.SemaphoreType.DMA(shape)
    grads, wgrad, gain_grad = pl.pallas_call(
        functools.partial(kernel, (ns, nt, nd)),
        out_shape=(
            jax.ShapeDtypeStruct((tokens, cols), bf16),
            jax.ShapeDtypeStruct((cols, cols), f32),
            jax.ShapeDtypeStruct((1, cols), f32),
        ),
        in_specs=[pl.BlockSpec(memory_space=pltpu.SMEM)] + [vmem] * 4,
        out_specs=(vmem, vmem, vmem),
        scratch_shapes=[
            pltpu.VMEM((nd, cols, cols), bf16),
            pltpu.VMEM((nt, tokens, cols + LANES), bf16),
            pltpu.VMEM((nt, tokens, cols), bf16),
            pltpu.VMEM((nt, tokens, cols), bf16),
            pltpu.VMEM((tokens, cols), bf16),
            pltpu.VMEM((nd, tokens, cols), bf16),
            pltpu.VMEM((nd, tokens, cols), bf16),
            pltpu.VMEM((tokens, cols), f32),
            pltpu.VMEM((tokens, cols), f32),
            pltpu.VMEM((tokens, cols + LANES), bf16),
            pltpu.VMEM((nt, tokens, LANES), f32),
            pltpu.VMEM((nt, tokens, LANES), bf16),
            pltpu.VMEM((nd, 8, cols), f32),
            dma(2, nd // 2, PIECES), dma(2, nd // 2, PIECES),
            dma(CHUNKS, nt), dma(CHUNKS, nt),
            dma(CHUNKS, nd), dma(CHUNKS, nd),
            dma(nt), dma(nt), dma(nt), dma(nt), dma(nd), dma(nd),
            dma(nt), dma(nt), dma(nd), dma(nd),
        ],
        compiler_params=pltpu.CompilerParams(
            collective_id=0, has_side_effects=True, vmem_limit_bytes=48 << 20
        ),
        name="relay",
    )(
        lengths,
        activations.reshape(tokens, cols),
        cotangent.reshape(tokens, cols),
        weights.reshape(cols, cols),
        gains,
    )
    return (
        grads.reshape(1, micro, seqlen, cols),
        wgrad.reshape(1, cols, cols),
        gain_grad,
    )


def solution(mesh):
    in_specs = (
        P("section", "dp", None, "tensor"),
        P("dp", None, "tensor"),
        P("dp"),
        P("section", "tensor", "dp"),
        P("section", "tensor"),
    )
    out_specs = (
        P("section", "dp", None, "tensor"),
        P("section", "tensor", "dp"),
        P("section", "tensor"),
    )
    return jax.shard_map(
        per_device, mesh=mesh, in_specs=in_specs, out_specs=out_specs, check_vma=False
    )
```

```python
import functools

import jax
import jax.numpy as jnp
from jax import lax
from jax.experimental import pallas as pl
from jax.experimental.pallas import tpu as pltpu
from jax.sharding import PartitionSpec as P

EPS = 1e-05
LANES = 128
CHUNKS = 4
WINDOW = 2
Q_PIECES = 2
TURN = 8
FINAL = 1
AHEAD = 2
PIECES = 4
MESH = pl.DeviceIdType.MESH


def remote(src, dst, send, recv, dev):
    return pltpu.make_async_remote_copy(
        src_ref=src, dst_ref=dst, send_sem=send, recv_sem=recv, device_id=dev, device_id_type=MESH
    )


def wide(tile, cols):
    return jnp.concatenate([tile] * (cols // LANES), axis=1)


class Ring:
    def __init__(self, buf, send, recv, d, nd, pieces, window):
        self.buf, self.send, self.recv = buf, send, recv
        self.d, self.nd, self.pieces, self.window = d, nd, pieces, window
        self.hops = nd // 2
        self.size = buf.shape[1] // pieces
        half = pieces // 2
        whole = [(hop, piece) for hop in range(1, self.hops) for piece in range(pieces)]
        self.order = {
            1: whole + [(self.hops, piece) for piece in range(half)],
            -1: whole + [(self.hops, piece) for piece in range(half, pieces)],
        }
        self.steps = len(self.order[1])

    def copy(self, block_hop, hop, piece, way):
        block = lax.rem(self.d - way * block_hop + 2 * self.nd, self.nd)
        view = self.buf.at[block, pl.ds(piece * self.size, self.size)]
        side = 0 if way > 0 else 1
        return remote(
            view, view, self.send.at[side, hop - 1, piece], self.recv.at[side, hop - 1, piece],
            {"dp": lax.rem(self.d + way + self.nd, self.nd)},
        )

    def left(self, i, way):
        hop, piece = self.order[way][i]
        self.copy(hop - 1, hop, piece, way).wait_send()

    def start(self, begin, end):
        for i in range(begin, end):
            for way in (1, -1):
                hop, piece = self.order[way][i]
                if hop > 1:
                    self.copy(hop - 1, hop - 1, piece, way).wait_recv()
                if i >= self.window:
                    self.left(i - self.window, way)
                self.copy(hop - 1, hop, piece, way).start()

    def finish(self):
        for way in (1, -1):
            for hop, piece in self.order[way]:
                if (hop + 1, piece) not in self.order[way]:
                    self.copy(hop, hop, piece, way).wait_recv()

    def drain(self):
        for i in range(max(self.steps - self.window, 0), self.steps):
            for way in (1, -1):
                self.left(i, way)


def kernel(
    sizes,
    lengths_ref, x_hbm, cot_hbm, w_hbm, gain_hbm,
    grads_out, wgrad_out, gain_out,
    x_ref, cot_ref, w_ref, gain_ref,
    w_all, inbox, grad_all, corr, corr_own, normed_all, swapped, xhat, upd, outbox,
    squares, rterm, gain_part, w_part, g_part, back_part, back_sent, back_in, back_now,
    in_sem, w_send, w_recv, q_send, q_recv, relay_send, relay_recv, swap_send, swap_recv,
    sq_send, sq_recv, corr_send, corr_recv, norm_send, norm_recv,
    r_send, r_recv, gn_send, gn_recv, quarter_send, quarter_recv, gq_send, gq_recv,
    back_send, back_recv, spread_send, cs_send, cross_send, cross_recv, turn, free,
):
    ns, nt, nd = sizes
    s, t, d = lax.axis_index("section"), lax.axis_index("tensor"), lax.axis_index("dp")
    tokens, cols = x_ref.shape
    width = cols * nt
    rows = tokens // CHUNKS
    seqlen = tokens // 2
    planes = ns // 2
    part_rows = cols // planes
    plane = s // 2
    first, last = s == ns - 1, s == 0
    odd = lax.rem(s, 2) == 1
    even = jnp.logical_not(odd)
    not_first, not_last = jnp.logical_not(first), jnp.logical_not(last)
    odd_inner = jnp.logical_and(odd, not_first)
    even_inner = jnp.logical_and(even, not_last)
    odd_late = jnp.logical_and(odd, s >= ns // 2)
    hurried = s == ns - 3
    final = s < FINAL
    not_final = jnp.logical_not(final)
    early = jnp.logical_not(odd_late)
    dp_peer = lambda k: lax.rem(d + k, nd)
    t_peer = lambda k: lax.rem(t + k, nt)

    loads = [
        pltpu.make_async_copy(src, dst, in_sem.at[n])
        for n, (src, dst) in enumerate(
            ((w_hbm, w_ref), (x_hbm, x_ref), (cot_hbm, cot_ref), (gain_hbm, gain_ref))
        )
    ]
    for load in loads:
        load.start()

    barrier = pltpu.get_barrier_semaphore()

    def greet(**where):
        pl.semaphore_signal(barrier, 1, device_id=where, device_id_type=MESH)

    for k in range(1, nd):
        greet(dp=dp_peer(k))
    for k in range(1, nt):
        greet(tensor=t_peer(k))

    @pl.when(not_last)
    def _():
        for k in range(nt):
            greet(section=s - 1, tensor=t_peer(k))

    @pl.when(not_first)
    def _():
        for k in range(nt):
            greet(section=s + 1, tensor=t_peer(k))

    @pl.when(odd_inner)
    def _():
        greet(section=ns - 1)

    @pl.when(first)
    def _():
        for p in range(planes - 1):
            greet(section=2 * p + 1)

    loads[0].wait()
    w_all[d] = w_ref[...].T
    loads[2].wait()

    def mask(m):
        def apply(value):
            position = lax.broadcasted_iota(jnp.int32, value.shape, 0)
            kept = jnp.where(position < lengths_ref[m], value.astype(jnp.float32), 0.0)
            return kept.astype(jnp.bfloat16)

        return apply

    @pl.when(odd)
    def _():
        mine = pl.ds(pl.multiple_of(plane * part_rows, part_rows), part_rows)
        for m in range(2):
            part = slice(m * seqlen, (m + 1) * seqlen)
            g_part[t, part] = mask(m)(cot_ref[part, mine])

    @pl.when(first)
    def _():
        w_part[d] = w_all[d, (planes - 1) * part_rows :]
        for m in range(2):
            part = slice(m * seqlen, (m + 1) * seqlen)
            inbox[t, part, :cols] = mask(m)(cot_ref[part])
        inbox[t, :, cols:] = jnp.zeros((tokens, LANES), jnp.bfloat16)

    loads[1].wait()
    loads[3].wait()
    x = x_ref[...].astype(jnp.float32)
    squares[t] = jnp.broadcast_to(jnp.sum(x * x, axis=1, keepdims=True), (tokens, LANES))

    expected = (
        nd - 1 + nt - 1
        + nt * (jnp.where(last, 0, 1) + jnp.where(first, 0, 1))
        + jnp.where(odd_inner, 1, 0) + jnp.where(first, planes - 1, 0)
    )
    pl.semaphore_wait(barrier, expected)

    whole = Ring(w_all, w_send, w_recv, d, nd, PIECES, WINDOW)
    quarter = Ring(w_part, q_send, q_recv, d, nd, Q_PIECES, 99)

    def quarter_copy(p):
        return remote(
            w_all.at[d, pl.ds(p * part_rows, part_rows)], w_part.at[d],
            quarter_send.at[p], quarter_recv, {"section": 2 * p + 1},
        )

    def gq_copy(k, src):
        return remote(
            g_part.at[src], g_part.at[src], gq_send.at[k], gq_recv.at[src], {"tensor": t_peer(k)}
        )

    def sq_copy(k, src):
        return remote(
            squares.at[src], squares.at[src], sq_send.at[k], sq_recv.at[src], {"tensor": t_peer(k)}
        )

    def spread_copy(c, k, src):
        view = pl.ds(pl.multiple_of(c * rows, rows), rows)
        return remote(
            inbox.at[src, view], inbox.at[src, view], spread_send.at[c, k], relay_recv.at[c, src],
            {"tensor": t_peer(k)},
        )

    def relay_copy(c, k, near):
        view = pl.ds(pl.multiple_of(c * rows, rows), rows)
        where = {"section": s - 1, "tensor": t_peer(k)} if near else {"section": s - 1}
        return remote(
            outbox.at[view], inbox.at[t, view], relay_send.at[c, k], relay_recv.at[c, t], where
        )

    def back_copy(c, p):
        view = pl.ds(c * rows, rows)
        return remote(
            back_sent.at[view], back_in.at[p, view], back_send.at[c], back_recv.at[c, p],
            {"section": ns - 1},
        )

    def corr_copy(k, near):
        where = {"section": s - 1, "tensor": t_peer(k)} if near else {"section": s - 1}
        return remote(corr_own, corr.at[t], corr_send.at[k], corr_recv.at[t], where)

    def corr_spread(k, src):
        return remote(
            corr.at[src], corr.at[src], cs_send.at[k], corr_recv.at[src], {"tensor": t_peer(k)}
        )

    def norm_copy(k, src):
        return remote(
            normed_all.at[src], normed_all.at[src], norm_send.at[k], norm_recv.at[src],
            {"dp": dp_peer(k)},
        )

    def swap_copy(c, k):
        view = pl.ds(pl.multiple_of(c * rows, rows), rows)
        return remote(
            grad_all.at[dp_peer(k), view], swapped.at[d, view], swap_send.at[c, k],
            swap_recv.at[c, d], {"dp": dp_peer(k)},
        )

    def slice_of(c):
        groups = cols // LANES
        height = rows // (nt // groups)
        mine = pl.ds(pl.multiple_of(c * rows + t // groups * height, height), height)
        return mine, pl.ds(pl.multiple_of(lax.rem(t, groups) * LANES, LANES), LANES)

    def slice_copy(c, k):
        mine, lanes = slice_of(c)
        return remote(
            grad_all.at[dp_peer(k), mine, lanes], swapped.at[d, mine, lanes], swap_send.at[c, k],
            swap_recv.at[c, d], {"dp": dp_peer(k)},
        )

    def cross_copy(c, k):
        mine, lanes = slice_of(c)
        view = swapped.at[:, mine, lanes]
        return remote(
            view, view, cross_send.at[c, k], cross_recv.at[c, t], {"tensor": t_peer(k)}
        )

    @pl.when(first)
    def _():
        for p in range(planes - 1):
            quarter_copy(p).start()

    @pl.when(hurried)
    def _():
        whole.start(0, PIECES // 2)

    @pl.when(s == ns - 2)
    def _():
        whole.start(0, PIECES)

    @pl.when(odd)
    def _():
        for k in range(1, nt):
            gq_copy(k, t).start()

    for k in range(1, nt):
        sq_copy(k, t).start()

    @pl.when(first)
    def _():
        quarter.start(0, Q_PIECES)
        corr[...] = jnp.zeros_like(corr)

    @pl.when(odd_inner)
    def _():
        quarter_copy(0).wait_recv()
        quarter.start(0, Q_PIECES)

    @pl.when(odd)
    def _():
        quarter.start(Q_PIECES, 2 * Q_PIECES)

    @pl.when(hurried)
    def _():
        whole.start(PIECES // 2, PIECES)

    gain = gain_ref[...].astype(jnp.float32)
    for k in range(1, nt):
        sq_copy(k, t_peer(k)).wait_recv()
    total = squares[0]
    for j in range(1, nt):
        total = total + squares[j]
    scale = wide(lax.rsqrt(total / width + EPS), cols)
    x = x_ref[...].astype(jnp.float32) * scale
    xhat[...] = x
    normed_all[d] = (x * gain).astype(jnp.bfloat16)
    corr_own[...] = (x * scale).astype(jnp.bfloat16)
    upd[...] = scale

    @pl.when(odd)
    def _():
        for k in range(nt):
            corr_copy(k, True).start()

    @pl.when(even_inner)
    def _():
        corr_copy(0, False).start()

    def pass_turn():
        pl.semaphore_signal(turn, 1, device_id={"section": s - 1}, device_id_type=MESH)

    @pl.when(odd)
    def _():
        quarter.start(2 * Q_PIECES, quarter.steps)

        @pl.when(first)
        def _():
            for c in range(CHUNKS):
                for k in range(1, nt):
                    spread_copy(c, k, t).start()

        @pl.when(hurried)
        def _():
            whole.start(PIECES, 2 * PIECES)

        @pl.when(jnp.logical_and(odd_inner, jnp.logical_not(hurried)))
        def _():
            whole.start(0, PIECES)

        quarter.finish()
        for k in range(1, nt):
            gq_copy(k, t_peer(k)).wait_recv()
        back = jnp.zeros((tokens, cols), jnp.float32)
        for j in range(nt):
            back = back + jnp.dot(g_part[j], w_part[j], preferred_element_type=jnp.float32)

        @pl.when(first)
        def _():
            back_part[...] = back

        @pl.when(not_first)
        def _():
            back_sent[...] = back.astype(jnp.bfloat16)
            for c in range(CHUNKS):
                back_copy(c, plane).start()
            @pl.when(jnp.logical_not(hurried))
            def _():
                whole.start(PIECES, 2 * PIECES)

            corr_spread(1, t).wait_recv()
            for k in range(1, nt):
                corr_spread(k, t).start()
            whole.start(2 * PIECES, TURN)
            pass_turn()
            whole.start(TURN, whole.steps)
            whole.finish()

    @pl.when(even)
    def _():
        @pl.when(s < ns - 2)
        def _():
            pl.semaphore_wait(turn, 1)
            whole.start(0, PIECES)

        whole.start(PIECES, whole.steps)
        pl.semaphore_signal(free, 1, device_id={"section": s + 1}, device_id_type=MESH)
        whole.finish()

    @pl.when(early)
    def _():
        @pl.when(odd)
        def _():
            pl.semaphore_wait(free, 1)

        for k in range(1, nd):
            norm_copy(k, d).start()

    @pl.when(not_first)
    def _():
        @pl.when(even)
        def _():
            corr_spread(1, t).wait_recv()

        for k in range(1, nt):
            corr_spread(k, t_peer(k)).wait_recv()

    gain_part[d] = jnp.zeros((8, cols), jnp.float32)

    def pass_on(c):
        @pl.when(jnp.logical_and(odd_inner, c < CHUNKS))
        def _():
            spread_copy(c, 1, t).wait_recv()
            for k in range(1, nt):
                spread_copy(c, k, t).start()

    def chunk(c, carry):
        view = pl.ds(pl.multiple_of(c * rows, rows), rows)

        pass_on(c + AHEAD)

        @pl.when(even)
        def _():
            spread_copy(c, 1, t).wait_recv()

        for k in range(1, nt):
            spread_copy(c, k, t_peer(k)).wait_recv()
        r = inbox[0, view, cols:].astype(jnp.float32)
        for j in range(1, nt):
            r = r + inbox[j, view, cols:].astype(jnp.float32)
        r = wide(r, cols)
        for j in range(nt):
            g = inbox[j, view, :cols].astype(jnp.float32) - corr[j, view].astype(jnp.float32) * r
            grad_all[j, view] = g.astype(jnp.bfloat16)

        @pl.when(first)
        def _():
            back = back_part[view]
            for p in range(planes - 1):
                remote(
                    back_sent.at[view], back_in.at[p, view], back_send.at[c], back_recv.at[c, p],
                    {"section": 1},
                ).wait_recv()
                back = back + back_in[p, view].astype(jnp.float32)
            back_now[...] = back

        @pl.when(not_first)
        def _():
            back = jnp.zeros((rows, cols), jnp.float32)
            for j in range(nt):
                back = back + jnp.dot(
                    grad_all[j, view], w_all[j], preferred_element_type=jnp.float32
                )
            back_now[...] = back

        back = back_now[...]
        xh = xhat[view]
        weighted = gain * back
        part = jnp.sum(weighted * xh, axis=1, keepdims=True) * (1.0 / width)
        u = grad_all[t, view].astype(jnp.float32) + upd[view] * weighted
        outbox[view, :cols] = u.astype(jnp.bfloat16)
        tile = jnp.broadcast_to(part, (rows, LANES)).astype(jnp.bfloat16)
        outbox[view, cols:] = tile

        @pl.when(odd)
        def _():
            for k in range(nt):
                relay_copy(c, k, True).start()

        @pl.when(even_inner)
        def _():
            relay_copy(c, 0, False).start()

        @pl.when(jnp.logical_and(early, not_final))
        def _():
            for k in range(1, nd):
                swap_copy(c, k).start()
            swapped[d, view] = grad_all[d, view]

        @pl.when(final)
        def _():
            for k in range(1, nd):
                slice_copy(c, k).start()
            mine, lanes = slice_of(c)
            swapped[d, mine, lanes] = grad_all[d, mine, lanes]

        upd[view] = u
        rterm[t, view] = tile
        gain_part[d] = gain_part[d] + jnp.sum((back * xh).reshape(rows // 8, 8, cols), axis=0)
        return carry

    for c in range(AHEAD):
        pass_on(c)
    lax.fori_loop(0, CHUNKS, chunk, 0)

    def r_copy(k, src):
        return remote(rterm.at[src], rterm.at[src], r_send.at[k], r_recv.at[src], {"tensor": t_peer(k)})

    def gn_copy(k, src):
        return remote(
            gain_part.at[src], gain_part.at[src], gn_send.at[k], gn_recv.at[src], {"dp": dp_peer(k)}
        )

    for k in range(1, nt):
        r_copy(k, t).start()

    @pl.when(odd_late)
    def _():
        pl.semaphore_wait(free, 1)
        for k in range(1, nd):
            norm_copy(k, d).start()
            for c in range(CHUNKS):
                swap_copy(c, k).start()
        swapped[d] = grad_all[d]

    @pl.when(final)
    def _():
        for c in range(CHUNKS):
            mine, lanes = slice_of(c)
            for k in range(1, nd):
                src = dp_peer(k)
                remote(
                    grad_all.at[src, mine, lanes], swapped.at[src, mine, lanes],
                    swap_send.at[c, k], swap_recv.at[c, src], {"dp": dp_peer(1)},
                ).wait_recv()
            for k in range(1, nt):
                cross_copy(c, k).start()

    for k in range(1, nd):
        gn_copy(k, d).start()
    for k in range(1, nt):
        r_copy(k, t_peer(k)).wait_recv()
    r = rterm[0].astype(jnp.float32)
    for j in range(1, nt):
        r = r + rterm[j].astype(jnp.float32)
    grads_out[...] = (
        upd[...] - corr_own[...].astype(jnp.float32) * wide(r, cols)
    ).astype(jnp.bfloat16)
    for k in range(1, nd):
        gn_copy(k, dp_peer(k)).wait_recv()
    sums = gain_part[0]
    for j in range(1, nd):
        sums = sums + gain_part[j]
    gain_out[...] = jnp.sum(sums, axis=0, keepdims=True)

    for k in range(1, nd):
        norm_copy(k, dp_peer(k)).wait_recv()

    @pl.when(not_final)
    def _():
        for k in range(1, nd):
            src = dp_peer(k)
            for c in range(CHUNKS):
                view = pl.ds(c * rows, rows)
                remote(
                    grad_all.at[src, view], swapped.at[src, view], swap_send.at[c, k],
                    swap_recv.at[c, src], {"dp": dp_peer(1)},
                ).wait_recv()

    @pl.when(final)
    def _():
        groups = cols // LANES
        height = rows // (nt // groups)
        for k in range(1, nt):
            src = t_peer(k)
            lanes = pl.ds(pl.multiple_of(lax.rem(src, groups) * LANES, LANES), LANES)
            for c in range(CHUNKS):
                theirs = pl.ds(pl.multiple_of(c * rows + src // groups * height, height), height)
                view = swapped.at[:, theirs, lanes]
                remote(
                    view, view, cross_send.at[c, k], cross_recv.at[c, src], {"tensor": t_peer(1)}
                ).wait_recv()

    acc = jnp.zeros((cols, cols), jnp.float32)
    for j in range(nd):
        acc = acc + lax.dot_general(
            normed_all[j], swapped[j], (((0,), (0,)), ((), ())), preferred_element_type=jnp.float32
        )
    wgrad_out[...] = acc

    for k in range(1, nt):
        sq_copy(k, t).wait_send()
        r_copy(k, t).wait_send()
    for k in range(1, nd):
        norm_copy(k, d).wait_send()
        gn_copy(k, d).wait_send()

    @pl.when(not_final)
    def _():
        for k in range(1, nd):
            for c in range(CHUNKS):
                swap_copy(c, k).wait_send()

    @pl.when(final)
    def _():
        for c in range(CHUNKS):
            for k in range(1, nd):
                slice_copy(c, k).wait_send()
            for k in range(1, nt):
                cross_copy(c, k).wait_send()

    @pl.when(not_first)
    def _():
        whole.drain()

    @pl.when(odd)
    def _():
        quarter.drain()
        for k in range(1, nt):
            gq_copy(k, t).wait_send()
            for c in range(CHUNKS):
                spread_copy(c, k, t).wait_send()
        for k in range(nt):
            for c in range(CHUNKS):
                relay_copy(c, k, True).wait_send()

    @pl.when(odd_inner)
    def _():
        for c in range(CHUNKS):
            back_copy(c, plane).wait_send()

    @pl.when(first)
    def _():
        for p in range(planes - 1):
            quarter_copy(p).wait_send()

    @pl.when(odd)
    def _():
        for k in range(nt):
            corr_copy(k, True).wait_send()

    @pl.when(odd_inner)
    def _():
        for k in range(1, nt):
            corr_spread(k, t).wait_send()

    @pl.when(even_inner)
    def _():
        corr_copy(0, False).wait_send()
        for c in range(CHUNKS):
            relay_copy(c, 0, False).wait_send()


def per_device(activations, cotangent, lengths, weights, gains):
    ns, nt, nd = (lax.axis_size(a) for a in ("section", "tensor", "dp"))
    _, micro, seqlen, cols = activations.shape
    tokens = micro * seqlen
    planes = ns // 2
    bf16, f32 = jnp.bfloat16, jnp.float32
    vmem = pl.BlockSpec(memory_space=pltpu.VMEM)
    hbm = pl.BlockSpec(memory_space=pl.ANY)
    dma = lambda *shape: pltpu.SemaphoreType.DMA(shape)
    ring = lambda pieces: dma(2, nd // 2, pieces)
    grads, wgrad, gain_grad = pl.pallas_call(
        functools.partial(kernel, (ns, nt, nd)),
        out_shape=(
            jax.ShapeDtypeStruct((tokens, cols), bf16),
            jax.ShapeDtypeStruct((cols, cols), f32),
            jax.ShapeDtypeStruct((1, cols), f32),
        ),
        in_specs=[pl.BlockSpec(memory_space=pltpu.SMEM)] + [hbm] * 4,
        out_specs=(vmem, vmem, vmem),
        scratch_shapes=[
            pltpu.VMEM((tokens, cols), bf16),
            pltpu.VMEM((tokens, cols), bf16),
            pltpu.VMEM((cols, cols), bf16),
            pltpu.VMEM((1, cols), bf16),
            pltpu.VMEM((nd, cols, cols), bf16),
            pltpu.VMEM((nt, tokens, cols + LANES), bf16),
            pltpu.VMEM((nt, tokens, cols), bf16),
            pltpu.VMEM((nt, tokens, cols), bf16),
            pltpu.VMEM((tokens, cols), bf16),
            pltpu.VMEM((nd, tokens, cols), bf16),
            pltpu.VMEM((nd, tokens, cols), bf16),
            pltpu.VMEM((tokens, cols), f32),
            pltpu.VMEM((tokens, cols), f32),
            pltpu.VMEM((tokens, cols + LANES), bf16),
            pltpu.VMEM((nt, tokens, LANES), f32),
            pltpu.VMEM((nt, tokens, LANES), bf16),
            pltpu.VMEM((nd, 8, cols), f32),
            pltpu.VMEM((nd, cols // planes, cols), bf16),
            pltpu.VMEM((nt, tokens, cols // planes), bf16),
            pltpu.VMEM((tokens, cols), f32),
            pltpu.VMEM((tokens, cols), bf16),
            pltpu.VMEM((planes - 1, tokens, cols), bf16),
            pltpu.VMEM((tokens // CHUNKS, cols), f32),
            dma(4),
            ring(PIECES), ring(PIECES), ring(Q_PIECES), ring(Q_PIECES),
            dma(CHUNKS, nt), dma(CHUNKS, nt),
            dma(CHUNKS, nd), dma(CHUNKS, nd),
            dma(nt), dma(nt), dma(nt), dma(nt), dma(nd), dma(nd),
            dma(nt), dma(nt), dma(nd), dma(nd),
            dma(planes), pltpu.SemaphoreType.DMA, dma(nt), dma(nt),
            dma(CHUNKS), dma(CHUNKS, planes), dma(CHUNKS, nt), dma(nt),
            dma(CHUNKS, nt), dma(CHUNKS, nt),
            pltpu.SemaphoreType.REGULAR, pltpu.SemaphoreType.REGULAR,
        ],
        compiler_params=pltpu.CompilerParams(
            collective_id=0, has_side_effects=True, vmem_limit_bytes=56 << 20
        ),
        name="relay",
    )(
        lengths,
        activations.reshape(tokens, cols),
        cotangent.reshape(tokens, cols),
        weights.reshape(cols, cols),
        gains,
    )
    return (
        grads.reshape(1, micro, seqlen, cols),
        wgrad.reshape(1, cols, cols),
        gain_grad,
    )


def solution(mesh):
    in_specs = (
        P("section", "dp", None, "tensor"),
        P("dp", None, "tensor"),
        P("dp"),
        P("section", "tensor", "dp"),
        P("section", "tensor"),
    )
    out_specs = (
        P("section", "dp", None, "tensor"),
        P("section", "tensor", "dp"),
        P("section", "tensor"),
    )
    return jax.shard_map(
        per_device, mesh=mesh, in_specs=in_specs, out_specs=out_specs, check_vma=False
    )
```

```python
import functools

import jax
import jax.numpy as jnp
from jax import lax
from jax.experimental import pallas as pl
from jax.experimental.pallas import tpu as pltpu
from jax.sharding import PartitionSpec as P

EPS = 1e-05
LANES = 128
CHUNKS = 4
WINDOW = 2
Q_PIECES = 2
TURN = 8
SPLIT = 2
AHEAD = 2
PIECES = 4
MESH = pl.DeviceIdType.MESH


def remote(src, dst, send, recv, dev):
    return pltpu.make_async_remote_copy(
        src_ref=src, dst_ref=dst, send_sem=send, recv_sem=recv, device_id=dev, device_id_type=MESH
    )


def wide(tile, cols):
    return jnp.concatenate([tile] * (cols // LANES), axis=1)


class Ring:
    def __init__(self, buf, send, recv, d, nd, pieces, window):
        self.buf, self.send, self.recv = buf, send, recv
        self.d, self.nd, self.pieces, self.window = d, nd, pieces, window
        self.hops = nd // 2
        self.size = buf.shape[1] // pieces
        half = pieces // 2
        whole = [(hop, piece) for hop in range(1, self.hops) for piece in range(pieces)]
        self.order = {
            1: whole + [(self.hops, piece) for piece in range(half)],
            -1: whole + [(self.hops, piece) for piece in range(half, pieces)],
        }
        self.steps = len(self.order[1])

    def copy(self, block_hop, hop, piece, way):
        block = lax.rem(self.d - way * block_hop + 2 * self.nd, self.nd)
        view = self.buf.at[block, pl.ds(piece * self.size, self.size)]
        side = 0 if way > 0 else 1
        return remote(
            view, view, self.send.at[side, hop - 1, piece], self.recv.at[side, hop - 1, piece],
            {"dp": lax.rem(self.d + way + self.nd, self.nd)},
        )

    def left(self, i, way):
        hop, piece = self.order[way][i]
        self.copy(hop - 1, hop, piece, way).wait_send()

    def start(self, begin, end):
        for i in range(begin, end):
            for way in (1, -1):
                hop, piece = self.order[way][i]
                if hop > 1:
                    self.copy(hop - 1, hop - 1, piece, way).wait_recv()
                if i >= self.window:
                    self.left(i - self.window, way)
                self.copy(hop - 1, hop, piece, way).start()

    def finish(self):
        for way in (1, -1):
            for hop, piece in self.order[way]:
                if (hop + 1, piece) not in self.order[way]:
                    self.copy(hop, hop, piece, way).wait_recv()

    def drain(self):
        for i in range(max(self.steps - self.window, 0), self.steps):
            for way in (1, -1):
                self.left(i, way)


def kernel(
    sizes,
    lengths_ref, x_hbm, cot_hbm, w_hbm, gain_hbm,
    grads_out, wgrad_out, gain_out,
    x_ref, cot_ref, w_ref, gain_ref,
    w_all, inbox, grad_all, corr, corr_own, normed_all, swapped, xhat, upd, outbox,
    squares, rterm, gain_part, w_part, g_part, back_part, back_sent, back_in, back_now,
    in_sem, w_send, w_recv, q_send, q_recv, relay_send, relay_recv, swap_send, swap_recv,
    sq_send, sq_recv, corr_send, corr_recv, norm_send, norm_recv,
    r_send, r_recv, gn_send, gn_recv, quarter_send, quarter_recv, gq_send, gq_recv,
    back_send, back_recv, spread_send, cs_send, cross_send, cross_recv, turn, free,
):
    ns, nt, nd = sizes
    s, t, d = lax.axis_index("section"), lax.axis_index("tensor"), lax.axis_index("dp")
    tokens, cols = x_ref.shape
    width = cols * nt
    rows = tokens // CHUNKS
    seqlen = tokens // 2
    planes = ns // 2
    part_rows = cols // planes
    plane = s // 2
    first, last = s == ns - 1, s == 0
    odd = lax.rem(s, 2) == 1
    even = jnp.logical_not(odd)
    not_first, not_last = jnp.logical_not(first), jnp.logical_not(last)
    odd_inner = jnp.logical_and(odd, not_first)
    even_inner = jnp.logical_and(even, not_last)
    odd_late = jnp.logical_and(odd, s >= ns // 2)
    hurried = s == ns - 3
    staged = lambda c: jnp.logical_or(last, jnp.logical_and(s == 1, c >= SPLIT))
    early = jnp.logical_not(odd_late)
    dp_peer = lambda k: lax.rem(d + k, nd)
    t_peer = lambda k: lax.rem(t + k, nt)

    loads = [
        pltpu.make_async_copy(src, dst, in_sem.at[n])
        for n, (src, dst) in enumerate(
            ((w_hbm, w_ref), (x_hbm, x_ref), (cot_hbm, cot_ref), (gain_hbm, gain_ref))
        )
    ]
    for load in loads:
        load.start()

    barrier = pltpu.get_barrier_semaphore()

    def greet(**where):
        pl.semaphore_signal(barrier, 1, device_id=where, device_id_type=MESH)

    for k in range(1, nd):
        greet(dp=dp_peer(k))
    for k in range(1, nt):
        greet(tensor=t_peer(k))

    @pl.when(not_last)
    def _():
        for k in range(nt):
            greet(section=s - 1, tensor=t_peer(k))

    @pl.when(not_first)
    def _():
        for k in range(nt):
            greet(section=s + 1, tensor=t_peer(k))

    @pl.when(odd_inner)
    def _():
        greet(section=ns - 1)

    @pl.when(first)
    def _():
        for p in range(planes - 1):
            greet(section=2 * p + 1)

    loads[0].wait()
    w_all[d] = w_ref[...].T
    loads[2].wait()

    def mask(m):
        def apply(value):
            position = lax.broadcasted_iota(jnp.int32, value.shape, 0)
            kept = jnp.where(position < lengths_ref[m], value.astype(jnp.float32), 0.0)
            return kept.astype(jnp.bfloat16)

        return apply

    @pl.when(odd)
    def _():
        mine = pl.ds(pl.multiple_of(plane * part_rows, part_rows), part_rows)
        for m in range(2):
            part = slice(m * seqlen, (m + 1) * seqlen)
            g_part[t, part] = mask(m)(cot_ref[part, mine])

    @pl.when(first)
    def _():
        w_part[d] = w_all[d, (planes - 1) * part_rows :]
        for m in range(2):
            part = slice(m * seqlen, (m + 1) * seqlen)
            inbox[t, part, :cols] = mask(m)(cot_ref[part])
        inbox[t, :, cols:] = jnp.zeros((tokens, LANES), jnp.bfloat16)

    loads[1].wait()
    loads[3].wait()
    x = x_ref[...].astype(jnp.float32)
    squares[t] = jnp.broadcast_to(jnp.sum(x * x, axis=1, keepdims=True), (tokens, LANES))

    expected = (
        nd - 1 + nt - 1
        + nt * (jnp.where(last, 0, 1) + jnp.where(first, 0, 1))
        + jnp.where(odd_inner, 1, 0) + jnp.where(first, planes - 1, 0)
    )
    pl.semaphore_wait(barrier, expected)

    whole = Ring(w_all, w_send, w_recv, d, nd, PIECES, WINDOW)
    quarter = Ring(w_part, q_send, q_recv, d, nd, Q_PIECES, 99)

    def quarter_copy(p):
        return remote(
            w_all.at[d, pl.ds(p * part_rows, part_rows)], w_part.at[d],
            quarter_send.at[p], quarter_recv, {"section": 2 * p + 1},
        )

    def gq_copy(k, src):
        return remote(
            g_part.at[src], g_part.at[src], gq_send.at[k], gq_recv.at[src], {"tensor": t_peer(k)}
        )

    def sq_copy(k, src):
        return remote(
            squares.at[src], squares.at[src], sq_send.at[k], sq_recv.at[src], {"tensor": t_peer(k)}
        )

    def spread_copy(c, k, src):
        view = pl.ds(pl.multiple_of(c * rows, rows), rows)
        return remote(
            inbox.at[src, view], inbox.at[src, view], spread_send.at[c, k], relay_recv.at[c, src],
            {"tensor": t_peer(k)},
        )

    def relay_copy(c, k, near):
        view = pl.ds(pl.multiple_of(c * rows, rows), rows)
        where = {"section": s - 1, "tensor": t_peer(k)} if near else {"section": s - 1}
        return remote(
            outbox.at[view], inbox.at[t, view], relay_send.at[c, k], relay_recv.at[c, t], where
        )

    def back_copy(c, p):
        view = pl.ds(c * rows, rows)
        return remote(
            back_sent.at[view], back_in.at[p, view], back_send.at[c], back_recv.at[c, p],
            {"section": ns - 1},
        )

    def corr_copy(k, near):
        where = {"section": s - 1, "tensor": t_peer(k)} if near else {"section": s - 1}
        return remote(corr_own, corr.at[t], corr_send.at[k], corr_recv.at[t], where)

    def corr_spread(k, src):
        return remote(
            corr.at[src], corr.at[src], cs_send.at[k], corr_recv.at[src], {"tensor": t_peer(k)}
        )

    def norm_copy(k, src):
        return remote(
            normed_all.at[src], normed_all.at[src], norm_send.at[k], norm_recv.at[src],
            {"dp": dp_peer(k)},
        )

    def swap_copy(c, k):
        view = pl.ds(pl.multiple_of(c * rows, rows), rows)
        return remote(
            grad_all.at[dp_peer(k), view], swapped.at[d, view], swap_send.at[c, k],
            swap_recv.at[c, d], {"dp": dp_peer(k)},
        )

    def slice_of(c):
        groups = cols // LANES
        height = rows // (nt // groups)
        mine = pl.ds(pl.multiple_of(c * rows + t // groups * height, height), height)
        return mine, pl.ds(pl.multiple_of(lax.rem(t, groups) * LANES, LANES), LANES)

    def slice_copy(c, k):
        mine, lanes = slice_of(c)
        return remote(
            grad_all.at[dp_peer(k), mine, lanes], swapped.at[d, mine, lanes], swap_send.at[c, k],
            swap_recv.at[c, d], {"dp": dp_peer(k)},
        )

    def cross_copy(c, k):
        mine, lanes = slice_of(c)
        view = swapped.at[:, mine, lanes]
        return remote(
            view, view, cross_send.at[c, k], cross_recv.at[c, t], {"tensor": t_peer(k)}
        )

    @pl.when(first)
    def _():
        for p in range(planes - 1):
            quarter_copy(p).start()

    @pl.when(hurried)
    def _():
        whole.start(0, PIECES // 2)

    @pl.when(s == ns - 2)
    def _():
        whole.start(0, PIECES)

    @pl.when(odd)
    def _():
        for k in range(1, nt):
            gq_copy(k, t).start()

    for k in range(1, nt):
        sq_copy(k, t).start()

    @pl.when(first)
    def _():
        quarter.start(0, Q_PIECES)
        corr[...] = jnp.zeros_like(corr)

    @pl.when(odd_inner)
    def _():
        quarter_copy(0).wait_recv()
        quarter.start(0, Q_PIECES)

    @pl.when(odd)
    def _():
        quarter.start(Q_PIECES, 2 * Q_PIECES)

    @pl.when(hurried)
    def _():
        whole.start(PIECES // 2, PIECES)

    gain = gain_ref[...].astype(jnp.float32)
    for k in range(1, nt):
        sq_copy(k, t_peer(k)).wait_recv()
    total = squares[0]
    for j in range(1, nt):
        total = total + squares[j]
    scale = wide(lax.rsqrt(total / width + EPS), cols)
    x = x_ref[...].astype(jnp.float32) * scale
    xhat[...] = x
    normed_all[d] = (x * gain).astype(jnp.bfloat16)
    corr_own[...] = (x * scale).astype(jnp.bfloat16)
    upd[...] = scale

    @pl.when(odd)
    def _():
        for k in range(nt):
            corr_copy(k, True).start()

    @pl.when(even_inner)
    def _():
        corr_copy(0, False).start()

    def pass_turn():
        pl.semaphore_signal(turn, 1, device_id={"section": s - 1}, device_id_type=MESH)

    @pl.when(odd)
    def _():
        quarter.start(2 * Q_PIECES, quarter.steps)

        @pl.when(first)
        def _():
            for c in range(CHUNKS):
                for k in range(1, nt):
                    spread_copy(c, k, t).start()

        @pl.when(hurried)
        def _():
            whole.start(PIECES, 2 * PIECES)

        @pl.when(jnp.logical_and(odd_inner, jnp.logical_not(hurried)))
        def _():
            whole.start(0, PIECES)

        quarter.finish()
        for k in range(1, nt):
            gq_copy(k, t_peer(k)).wait_recv()
        back = jnp.zeros((tokens, cols), jnp.float32)
        for j in range(nt):
            back = back + jnp.dot(g_part[j], w_part[j], preferred_element_type=jnp.float32)

        @pl.when(first)
        def _():
            back_part[...] = back

        @pl.when(not_first)
        def _():
            back_sent[...] = back.astype(jnp.bfloat16)
            for c in range(CHUNKS):
                back_copy(c, plane).start()
            @pl.when(jnp.logical_not(hurried))
            def _():
                whole.start(PIECES, 2 * PIECES)

            corr_spread(1, t).wait_recv()
            for k in range(1, nt):
                corr_spread(k, t).start()
            whole.start(2 * PIECES, TURN)
            pass_turn()
            whole.start(TURN, whole.steps)
            whole.finish()

    @pl.when(even)
    def _():
        @pl.when(s < ns - 2)
        def _():
            pl.semaphore_wait(turn, 1)
            whole.start(0, PIECES)

        whole.start(PIECES, whole.steps)
        pl.semaphore_signal(free, 1, device_id={"section": s + 1}, device_id_type=MESH)
        whole.finish()

    @pl.when(early)
    def _():
        @pl.when(odd)
        def _():
            pl.semaphore_wait(free, 1)

        for k in range(1, nd):
            norm_copy(k, d).start()

    @pl.when(not_first)
    def _():
        @pl.when(even)
        def _():
            corr_spread(1, t).wait_recv()

        for k in range(1, nt):
            corr_spread(k, t_peer(k)).wait_recv()

    gain_part[d] = jnp.zeros((8, cols), jnp.float32)

    def pass_on(c):
        @pl.when(jnp.logical_and(odd_inner, c < CHUNKS))
        def _():
            spread_copy(c, 1, t).wait_recv()
            for k in range(1, nt):
                spread_copy(c, k, t).start()

    def chunk(c, carry):
        view = pl.ds(pl.multiple_of(c * rows, rows), rows)

        pass_on(c + AHEAD)

        @pl.when(even)
        def _():
            spread_copy(c, 1, t).wait_recv()

        for k in range(1, nt):
            spread_copy(c, k, t_peer(k)).wait_recv()
        r = inbox[0, view, cols:].astype(jnp.float32)
        for j in range(1, nt):
            r = r + inbox[j, view, cols:].astype(jnp.float32)
        r = wide(r, cols)
        for j in range(nt):
            g = inbox[j, view, :cols].astype(jnp.float32) - corr[j, view].astype(jnp.float32) * r
            grad_all[j, view] = g.astype(jnp.bfloat16)

        @pl.when(first)
        def _():
            back = back_part[view]
            for p in range(planes - 1):
                remote(
                    back_sent.at[view], back_in.at[p, view], back_send.at[c], back_recv.at[c, p],
                    {"section": 1},
                ).wait_recv()
                back = back + back_in[p, view].astype(jnp.float32)
            back_now[...] = back

        @pl.when(not_first)
        def _():
            back = jnp.zeros((rows, cols), jnp.float32)
            for j in range(nt):
                back = back + jnp.dot(
                    grad_all[j, view], w_all[j], preferred_element_type=jnp.float32
                )
            back_now[...] = back

        back = back_now[...]
        xh = xhat[view]
        weighted = gain * back
        part = jnp.sum(weighted * xh, axis=1, keepdims=True) * (1.0 / width)
        u = grad_all[t, view].astype(jnp.float32) + upd[view] * weighted
        outbox[view, :cols] = u.astype(jnp.bfloat16)
        tile = jnp.broadcast_to(part, (rows, LANES)).astype(jnp.bfloat16)
        outbox[view, cols:] = tile

        @pl.when(odd)
        def _():
            for k in range(nt):
                relay_copy(c, k, True).start()

        @pl.when(even_inner)
        def _():
            relay_copy(c, 0, False).start()

        @pl.when(jnp.logical_and(early, jnp.logical_not(staged(c))))
        def _():
            for k in range(1, nd):
                swap_copy(c, k).start()
            swapped[d, view] = grad_all[d, view]

        @pl.when(staged(c))
        def _():
            for k in range(1, nd):
                slice_copy(c, k).start()
            mine, lanes = slice_of(c)
            swapped[d, mine, lanes] = grad_all[d, mine, lanes]

        upd[view] = u
        rterm[t, view] = tile
        gain_part[d] = gain_part[d] + jnp.sum((back * xh).reshape(rows // 8, 8, cols), axis=0)
        return carry

    for c in range(AHEAD):
        pass_on(c)
    lax.fori_loop(0, CHUNKS, chunk, 0)

    def r_copy(k, src):
        return remote(rterm.at[src], rterm.at[src], r_send.at[k], r_recv.at[src], {"tensor": t_peer(k)})

    def gn_copy(k, src):
        return remote(
            gain_part.at[src], gain_part.at[src], gn_send.at[k], gn_recv.at[src], {"dp": dp_peer(k)}
        )

    for k in range(1, nt):
        r_copy(k, t).start()

    @pl.when(odd_late)
    def _():
        pl.semaphore_wait(free, 1)
        for k in range(1, nd):
            norm_copy(k, d).start()
            for c in range(CHUNKS):
                swap_copy(c, k).start()
        swapped[d] = grad_all[d]

    for c in range(CHUNKS):

        @pl.when(staged(c))
        def _():
            mine, lanes = slice_of(c)
            for k in range(1, nd):
                src = dp_peer(k)
                remote(
                    grad_all.at[src, mine, lanes], swapped.at[src, mine, lanes],
                    swap_send.at[c, k], swap_recv.at[c, src], {"dp": dp_peer(1)},
                ).wait_recv()
            for k in range(1, nt):
                cross_copy(c, k).start()

    for k in range(1, nd):
        gn_copy(k, d).start()
    for k in range(1, nt):
        r_copy(k, t_peer(k)).wait_recv()
    r = rterm[0].astype(jnp.float32)
    for j in range(1, nt):
        r = r + rterm[j].astype(jnp.float32)
    grads_out[...] = (
        upd[...] - corr_own[...].astype(jnp.float32) * wide(r, cols)
    ).astype(jnp.bfloat16)
    for k in range(1, nd):
        gn_copy(k, dp_peer(k)).wait_recv()
    sums = gain_part[0]
    for j in range(1, nd):
        sums = sums + gain_part[j]
    gain_out[...] = jnp.sum(sums, axis=0, keepdims=True)

    for k in range(1, nd):
        norm_copy(k, dp_peer(k)).wait_recv()

    groups = cols // LANES
    height = rows // (nt // groups)
    for c in range(CHUNKS):

        @pl.when(jnp.logical_not(staged(c)))
        def _():
            for k in range(1, nd):
                src = dp_peer(k)
                view = pl.ds(c * rows, rows)
                remote(
                    grad_all.at[src, view], swapped.at[src, view], swap_send.at[c, k],
                    swap_recv.at[c, src], {"dp": dp_peer(1)},
                ).wait_recv()

        @pl.when(staged(c))
        def _():
            for k in range(1, nt):
                src = t_peer(k)
                lanes = pl.ds(pl.multiple_of(lax.rem(src, groups) * LANES, LANES), LANES)
                theirs = pl.ds(pl.multiple_of(c * rows + src // groups * height, height), height)
                view = swapped.at[:, theirs, lanes]
                remote(
                    view, view, cross_send.at[c, k], cross_recv.at[c, src], {"tensor": t_peer(1)}
                ).wait_recv()

    acc = jnp.zeros((cols, cols), jnp.float32)
    for j in range(nd):
        acc = acc + lax.dot_general(
            normed_all[j], swapped[j], (((0,), (0,)), ((), ())), preferred_element_type=jnp.float32
        )
    wgrad_out[...] = acc

    for k in range(1, nt):
        sq_copy(k, t).wait_send()
        r_copy(k, t).wait_send()
    for k in range(1, nd):
        norm_copy(k, d).wait_send()
        gn_copy(k, d).wait_send()

    for c in range(CHUNKS):

        @pl.when(jnp.logical_not(staged(c)))
        def _():
            for k in range(1, nd):
                swap_copy(c, k).wait_send()

        @pl.when(staged(c))
        def _():
            for k in range(1, nd):
                slice_copy(c, k).wait_send()
            for k in range(1, nt):
                cross_copy(c, k).wait_send()

    @pl.when(not_first)
    def _():
        whole.drain()

    @pl.when(odd)
    def _():
        quarter.drain()
        for k in range(1, nt):
            gq_copy(k, t).wait_send()
            for c in range(CHUNKS):
                spread_copy(c, k, t).wait_send()
        for k in range(nt):
            for c in range(CHUNKS):
                relay_copy(c, k, True).wait_send()

    @pl.when(odd_inner)
    def _():
        for c in range(CHUNKS):
            back_copy(c, plane).wait_send()

    @pl.when(first)
    def _():
        for p in range(planes - 1):
            quarter_copy(p).wait_send()

    @pl.when(odd)
    def _():
        for k in range(nt):
            corr_copy(k, True).wait_send()

    @pl.when(odd_inner)
    def _():
        for k in range(1, nt):
            corr_spread(k, t).wait_send()

    @pl.when(even_inner)
    def _():
        corr_copy(0, False).wait_send()
        for c in range(CHUNKS):
            relay_copy(c, 0, False).wait_send()


def copy_out(a, b, c, a_out, b_out, c_out):
    a_out[...] = a[...]
    b_out[...] = b[...]
    c_out[...] = c[...]


def per_device(activations, cotangent, lengths, weights, gains):
    ns, nt, nd = (lax.axis_size(a) for a in ("section", "tensor", "dp"))
    _, micro, seqlen, cols = activations.shape
    tokens = micro * seqlen
    planes = ns // 2
    bf16, f32 = jnp.bfloat16, jnp.float32
    vmem = pl.BlockSpec(memory_space=pltpu.VMEM)
    hbm = pl.BlockSpec(memory_space=pl.ANY)
    dma = lambda *shape: pltpu.SemaphoreType.DMA(shape)
    ring = lambda pieces: dma(2, nd // 2, pieces)
    grads, wgrad, gain_grad = pl.pallas_call(
        functools.partial(kernel, (ns, nt, nd)),
        out_shape=(
            jax.ShapeDtypeStruct((tokens, cols), bf16),
            jax.ShapeDtypeStruct((cols, cols), f32),
            jax.ShapeDtypeStruct((1, cols), f32),
        ),
        in_specs=[pl.BlockSpec(memory_space=pltpu.SMEM)] + [hbm] * 4,
        out_specs=(vmem, vmem, vmem),
        scratch_shapes=[
            pltpu.VMEM((tokens, cols), bf16),
            pltpu.VMEM((tokens, cols), bf16),
            pltpu.VMEM((cols, cols), bf16),
            pltpu.VMEM((1, cols), bf16),
            pltpu.VMEM((nd, cols, cols), bf16),
            pltpu.VMEM((nt, tokens, cols + LANES), bf16),
            pltpu.VMEM((nt, tokens, cols), bf16),
            pltpu.VMEM((nt, tokens, cols), bf16),
            pltpu.VMEM((tokens, cols), bf16),
            pltpu.VMEM((nd, tokens, cols), bf16),
            pltpu.VMEM((nd, tokens, cols), bf16),
            pltpu.VMEM((tokens, cols), f32),
            pltpu.VMEM((tokens, cols), f32),
            pltpu.VMEM((tokens, cols + LANES), bf16),
            pltpu.VMEM((nt, tokens, LANES), f32),
            pltpu.VMEM((nt, tokens, LANES), bf16),
            pltpu.VMEM((nd, 8, cols), f32),
            pltpu.VMEM((nd, cols // planes, cols), bf16),
            pltpu.VMEM((nt, tokens, cols // planes), bf16),
            pltpu.VMEM((tokens, cols), f32),
            pltpu.VMEM((tokens, cols), bf16),
            pltpu.VMEM((planes - 1, tokens, cols), bf16),
            pltpu.VMEM((tokens // CHUNKS, cols), f32),
            dma(4),
            ring(PIECES), ring(PIECES), ring(Q_PIECES), ring(Q_PIECES),
            dma(CHUNKS, nt), dma(CHUNKS, nt),
            dma(CHUNKS, nd), dma(CHUNKS, nd),
            dma(nt), dma(nt), dma(nt), dma(nt), dma(nd), dma(nd),
            dma(nt), dma(nt), dma(nd), dma(nd),
            dma(planes), pltpu.SemaphoreType.DMA, dma(nt), dma(nt),
            dma(CHUNKS), dma(CHUNKS, planes), dma(CHUNKS, nt), dma(nt),
            dma(CHUNKS, nt), dma(CHUNKS, nt),
            pltpu.SemaphoreType.REGULAR, pltpu.SemaphoreType.REGULAR,
        ],
        compiler_params=pltpu.CompilerParams(
            collective_id=0, has_side_effects=True, vmem_limit_bytes=56 << 20
        ),
        name="relay",
    )(
        lengths,
        activations.reshape(tokens, cols),
        cotangent.reshape(tokens, cols),
        weights.reshape(cols, cols),
        gains,
    )
    grads, wgrad, gain_grad = pl.pallas_call(
        copy_out,
        out_shape=(
            jax.ShapeDtypeStruct((tokens, cols), bf16),
            jax.ShapeDtypeStruct((cols, cols), f32),
            jax.ShapeDtypeStruct((1, cols), f32),
        ),
        grid=(4,),
        in_specs=[
            pl.BlockSpec((tokens // 4, cols), lambda i: (i, 0)),
            pl.BlockSpec((cols // 4, cols), lambda i: (i, 0)),
            pl.BlockSpec((1, cols), lambda i: (0, 0)),
        ],
        out_specs=(
            pl.BlockSpec((tokens // 4, cols), lambda i: (i, 0)),
            pl.BlockSpec((cols // 4, cols), lambda i: (i, 0)),
            pl.BlockSpec((1, cols), lambda i: (0, 0)),
        ),
        name="copy_out",
    )(grads, wgrad, gain_grad)
    return (
        grads.reshape(1, micro, seqlen, cols),
        wgrad.reshape(1, cols, cols),
        gain_grad,
    )


def solution(mesh):
    in_specs = (
        P("section", "dp", None, "tensor"),
        P("dp", None, "tensor"),
        P("dp"),
        P("section", "tensor", "dp"),
        P("section", "tensor"),
    )
    out_specs = (
        P("section", "dp", None, "tensor"),
        P("section", "tensor", "dp"),
        P("section", "tensor"),
    )
    return jax.shard_map(
        per_device, mesh=mesh, in_specs=in_specs, out_specs=out_specs, check_vma=False
    )
```
